32 devices in a mesh: grp: 2 (over x), row: 16 (over z, y, core).
Axes of the slice: x: 2, y: 2, z: 4, core: 2. Of those that a mesh axis runs over, the one named last changes fastest.
Arguments:
- blocks: float32 [1024, 7, 6, 6, 128], P(('grp', 'row')), parts along dimension 0, may hold values from -0.3 to 4.2
- couplings: int32 [1024, 4], P(('grp', 'row')), parts along dimension 0, may hold values from -1 to 511, as said below
- cotangent: float32 [1024, 6, 128], P(('grp', 'row')), parts along dimension 0, may hold values from -7.2 to 7.2
Outputs:
- adjoint: float32 [1024, 6, 128], P(('grp', 'row')), parts along dimension 0
- residual: float32 [1024, 6, 128], P(('grp', 'row')), parts along dimension 0
The draws below stay inside these ranges and needn't reach their ends.
There are 2 independent parts, one for each index of `grp`. The reference program is written for one: setup_inputs(seed, part) draws one part's arguments, and reference() takes and returns one part's arrays. A program takes and returns all parts, laid end to end along the dimension named above; each array names one. Nothing has to cross between parts.
Inputs may be any that keep to these rules, and one draw needn't show every extreme that they name: With the device of tile t being t // 32: column 0 holds a tile of the next device, column 1 one of the previous device, column 2 one of the device 2 ahead, column 3 one of the device 2 behind; -1 exactly where that device lies outside the plate. Each column maps the tiles of one device one-to-one onto the tiles of its target device, and for s = couplings[t, k] >= 0, couplings[s, k'] = t, where k' pairs column 0 with 1 and 2 with 3.
All inputs are finite; a program needn't handle non-finite values.
Results may differ from the reference program's by a relative error of at most 0.0003.
Values sent between devices are 32-bit elements; how exact they have to be, the bound alone decides.
A program may use at most 64 MiB of HBM per device.

```python
import jax
import jax.numpy as jnp

TILES_DEV = 32
TILE = 128
FIELDS = 6
ITERS = 2
NT = 512


def draw_couplings(key, part):
    key = jax.random.fold_in(key, 11)
    tile_count = TILES_DEV
    device_count = NT // tile_count
    far_reach = max(2, device_count // 8)
    device_ids = jnp.arange(device_count, dtype=jnp.int32)[:, None]
    local_ids = jnp.arange(tile_count, dtype=jnp.int32)
    columns = []
    for pass_index, reach in enumerate((1, far_reach)):
        pass_keys = jax.random.split(jax.random.fold_in(key, pass_index), device_count)
        perms = jax.vmap(lambda one_key: jax.random.permutation(one_key, tile_count).astype(jnp.int32))(pass_keys)
        inverse = jax.vmap(lambda order: jnp.zeros((tile_count,), jnp.int32).at[order].set(local_ids))(perms)
        ahead_dev = device_ids + reach
        ahead = jnp.where(ahead_dev < device_count, ahead_dev * tile_count + perms, -1)
        behind_dev = device_ids - reach
        source_rows = jnp.clip(jnp.arange(device_count, dtype=jnp.int32) - reach, 0, device_count - 1)
        behind = jnp.where(behind_dev >= 0, behind_dev * tile_count + inverse[source_rows], -1)
        columns.append(ahead.reshape(NT))
        columns.append(behind.reshape(NT))
    return jnp.stack(columns, axis=1).astype(jnp.int32)


def draw_blocks(key, part):
    key = jax.random.fold_in(key, 23)
    main_key, diag_key = jax.random.split(key)
    shape = (NT, 7, FIELDS, FIELDS, TILE)
    spread = jax.random.uniform(main_key, shape, jnp.float32, -0.17, 0.17)
    leading = jax.random.uniform(diag_key, (NT, FIELDS, TILE), jnp.float32, 2.0, 4.0)
    slot_ids = jnp.arange(7)[:, None, None, None]
    row_ids = jnp.arange(FIELDS)[None, :, None, None]
    col_ids = jnp.arange(FIELDS)[None, None, :, None]
    diagonal = ((slot_ids == 0) & (row_ids == col_ids)).astype(jnp.float32)[None]
    return spread * (1.0 - diagonal) + diagonal * leading[:, None, :, None, :]


def draw_cotangent(key, part):
    key = jax.random.fold_in(key, 37)
    tile_pos = jnp.arange(NT, dtype=jnp.float32)[:, None, None] / max(NT - 1, 1)
    shape = (NT, FIELDS, TILE)
    values = jnp.clip(jax.random.normal(key, shape, jnp.float32), -4.0, 4.0)
    return 0.6 * values * 3.0 ** tile_pos


def setup_inputs(seed: int = 0, part: int = 0) -> dict:
    streams_of = jax.random.split(jax.random.key(seed), 4)
    part_splits = jax.random.split(jax.random.fold_in(streams_of[3], part), 4)
    blocks = draw_blocks(jax.random.fold_in(jax.random.fold_in(streams_of[3], part), 71), part)
    couplings = draw_couplings(jax.random.fold_in(jax.random.fold_in(streams_of[3], part), 71), part)
    cotangent = draw_cotangent(jax.random.fold_in(jax.random.fold_in(streams_of[3], part), 71), part)
    return dict(blocks=blocks, couplings=couplings, cotangent=cotangent)


def before_cell(values):
    last_cells = values[..., -1]
    moved = jnp.concatenate([jnp.zeros_like(last_cells[:1]), last_cells[:-1]], axis=0)
    return jnp.concatenate([moved[..., None], values[..., :-1]], axis=-1)


def after_cell(values):
    first_cells = values[..., 0]
    moved = jnp.concatenate([first_cells[1:], jnp.zeros_like(first_cells[:1])], axis=0)
    return jnp.concatenate([values[..., 1:], moved[..., None]], axis=-1)


def flip_blocks(blocks, couplings):
    paired = [1, 0, 3, 2]
    slots = [blocks[:, 0], before_cell(blocks[:, 2]), after_cell(blocks[:, 1])]
    present_cols = couplings >= 0
    safe_cols = jnp.where(present_cols, couplings, 0).astype(jnp.int32)
    for column in range(4):
        picked = blocks[safe_cols[:, column], 3 + paired[column]]
        slots.append(jnp.where(present_cols[:, column, None, None, None], picked, 0.0))
    return jnp.swapaxes(jnp.stack(slots, axis=1), 2, 3), safe_cols, present_cols


def apply_adjoint(transposed, safe_cols, present_cols, field):
    nearby = [field, before_cell(field), after_cell(field)]
    for column in range(4):
        nearby.append(jnp.where(present_cols[:, column, None, None], field[safe_cols[:, column]], 0.0))
    stacked = jnp.stack(nearby, axis=1)
    return jnp.sum(transposed * stacked[:, :, None], axis=(1, 3))


def reference(blocks, couplings, cotangent):
    transposed, safe_cols, present_cols = flip_blocks(blocks, couplings)
    adjoint = jnp.zeros_like(cotangent)
    residual = cotangent
    shadow = cotangent
    direction = cotangent
    rho_now = jnp.sum(shadow * residual)
    for iteration in range(ITERS):
        image_dir = apply_adjoint(transposed, safe_cols, present_cols, direction)
        alpha_step = rho_now / jnp.sum(shadow * image_dir)
        half_step = residual - alpha_step * image_dir
        bent_image = apply_adjoint(transposed, safe_cols, present_cols, half_step)
        omega_step = jnp.sum(bent_image * half_step) / jnp.sum(bent_image * bent_image)
        adjoint = adjoint + alpha_step * direction + omega_step * half_step
        residual = half_step - omega_step * bent_image
        if iteration + 1 < ITERS:
            rho_next = jnp.sum(shadow * residual)
            direction = residual + (rho_next / rho_now) * (alpha_step / omega_step) * (direction - omega_step * image_dir)
            rho_now = rho_next
    return adjoint, residual
```

```python
import functools

import jax
import jax.numpy as jnp
from jax import lax
from jax.experimental import pallas as pl
from jax.experimental.pallas import tpu as pltpu
from jax.sharding import PartitionSpec as P

MESH = pl.DeviceIdType.MESH
PAIRED = (1, 0, 3, 2)
ORDER = (2, 3, 0, 1)
GROUP = 8


def kernel(
    n, far, blocks_hbm, coup, b_ref, adj_ref, res_ref,
    blk, edge_blk, img, img2, bent, bent_img, direc, half,
    left, right, send, red_send, red,
    load_sem, send_sem, recv_sem, red_send_sem, red_recv_sem, *arrivals,
):
    recv = [arrivals[4 * step:4 * step + 4] for step in range(4)]
    tiles, fields, cells = b_ref.shape
    me = lax.axis_index("row")
    offsets = (1, -1, far, -far)
    last = tiles - 1

    def load(slot):
        return pltpu.make_async_copy(blocks_hbm.at[:, slot], blk.at[slot], load_sem.at[slot])

    edge_loads = (
        pltpu.make_async_copy(blocks_hbm.at[last, 2], edge_blk.at[0], load_sem.at[7]),
        pltpu.make_async_copy(blocks_hbm.at[0, 1], edge_blk.at[1], load_sem.at[8]),
    )
    load(5).start()
    load(6).start()
    edge_loads[0].start()
    edge_loads[1].start()
    for slot in (3, 4, 1, 2, 0):
        load(slot).start()

    barrier = pltpu.get_barrier_semaphore()

    def greet(i, carry):
        other = lax.rem(me + i, n)
        pl.semaphore_signal(barrier, inc=1, device_id={"row": other}, device_id_type=MESH)
        return carry

    lax.fori_loop(1, n, greet, 0)

    def has_target(j):
        to = me + offsets[j]
        return jnp.logical_and(to >= 0, to < n)

    def has_source(j):
        origin = me - offsets[j]
        return jnp.logical_and(origin >= 0, origin < n)

    for j in range(4):
        @pl.when(jnp.logical_not(has_source(j)))
        def _():
            for step in range(4):
                recv[step][j][...] = jnp.zeros(recv[step][j].shape, jnp.float32)

    def message(step, j):
        return pltpu.make_async_remote_copy(
            src_ref=send.at[step, j],
            dst_ref=recv[step][j],
            send_sem=send_sem.at[step, j],
            recv_sem=recv_sem.at[step, j],
            device_id={"row": me + offsets[j]},
            device_id_type=MESH,
        )

    lane = lax.broadcasted_iota(jnp.int32, (fields, cells), 1)
    first_lane = lane == 0
    last_lane = lane == cells - 1

    def product(field, slot, rows):
        total = None
        for a in range(fields):
            term = blk[slot, rows, a] * field[rows, pl.ds(a, 1), :]
            total = term if total is None else total + term
        return total

    def edge_product(field, which, tile):
        total = None
        for a in range(fields):
            term = edge_blk[which, a] * field[tile, pl.ds(a, 1), :]
            total = term if total is None else total + term
        return total

    def send_channels(step, field):
        for j in ORDER:
            if step == 0:
                load(3 + j).wait()

            @pl.loop(0, tiles // GROUP)
            def _(chunk):
                rows = pl.ds(chunk * GROUP, GROUP)
                send[step, j, rows] = product(field, 3 + j, rows)

            if j < 2:
                if step == 0:
                    edge_loads[j].wait()
                edge = edge_product(field, j, last if j == 0 else 0)
                send[step, j, tiles] = pltpu.roll(edge, 1 if j == 0 else cells - 1, 1)
            else:
                send[step, j, tiles] = jnp.zeros((fields, cells), jnp.float32)
            if step == 0 and j == ORDER[0]:
                pl.semaphore_wait(barrier, n - 1)

            @pl.when(has_target(j))
            def _():
                message(step, j).start()

    def local_part(step, field, out):
        if step == 0:
            for slot in (1, 2, 0):
                load(slot).wait()
            left[tiles] = jnp.zeros((fields, cells), jnp.float32)
            right[0] = jnp.zeros((fields, cells), jnp.float32)

        @pl.loop(0, tiles // GROUP)
        def _(chunk):
            rows = pl.ds(chunk * GROUP, GROUP)
            left[rows] = pltpu.roll(product(field, 1, rows), cells - 1, 2)
            right[pl.ds(chunk * GROUP + 1, GROUP)] = pltpu.roll(product(field, 2, rows), 1, 2)
            out[rows] = product(field, 0, rows)

        @pl.loop(0, tiles // GROUP)
        def _(chunk):
            rows = pl.ds(chunk * GROUP, GROUP)
            after = pl.ds(chunk * GROUP + 1, GROUP)
            out[rows] = (
                out[rows]
                + jnp.where(last_lane, left[after], left[rows])
                + jnp.where(first_lane, right[rows], right[after])
            )

    def receive(step, out):
        for j in ORDER:
            @pl.when(has_source(j))
            def _():
                message(step, j).wait_recv()

            @pl.loop(0, tiles // GROUP)
            def _(chunk):
                for i in range(GROUP):
                    tile = chunk * GROUP + i
                    origin = jnp.bitwise_and(coup[tile, PAIRED[j]], tiles - 1)
                    out[tile] = out[tile] + recv[step][j][origin]

        out[0] = out[0] + jnp.where(first_lane, recv[step][0][tiles], 0.0)
        out[last] = out[last] + jnp.where(last_lane, recv[step][1][tiles], 0.0)

    def partial_copy(step, other, origin):
        return pltpu.make_async_remote_copy(
            src_ref=red_send.at[step],
            dst_ref=red.at[step, origin],
            send_sem=red_send_sem.at[step, other],
            recv_sem=red_recv_sem.at[step, origin],
            device_id={"row": other},
            device_id_type=MESH,
        )

    def share(step, pairs):
        rows = [
            jnp.sum(jnp.sum(x * y, axis=0), axis=0, keepdims=True) for x, y in pairs
        ]
        rows += [jnp.zeros((8 - len(rows), cells), jnp.float32)]
        tile = jnp.concatenate(rows, axis=0)
        red_send[step] = tile
        red[step, me] = tile

        def go(i, carry):
            partial_copy(step, lax.rem(me + i, n), me).start()
            return carry

        lax.fori_loop(1, n, go, 0)

    def collect(step, count):
        def arrive(i, carry):
            other = lax.rem(me + i, n)
            partial_copy(step, other, other).wait_recv()
            return carry

        lax.fori_loop(1, n, arrive, 0)
        total = jnp.sum(jnp.sum(red[step], axis=0), axis=1, keepdims=True)
        return [total[q:q + 1] for q in range(count)]

    send_channels(0, b_ref)
    local_part(0, b_ref, img)
    receive(0, img)
    b = b_ref[...]
    share(0, [(b, b), (b, img[...])])

    send_channels(1, img)
    local_part(1, img, img2)
    rho, shadow_image = collect(0, 2)
    alpha = rho / shadow_image
    receive(1, img2)
    half[...] = b_ref[...] - alpha * img[...]
    bent[...] = img[...] - alpha * img2[...]
    share(1, [
        (bent[...], half[...]), (bent[...], bent[...]),
        (b_ref[...], bent[...]), (b_ref[...], half[...]),
    ])

    send_channels(2, bent)
    local_part(2, bent, bent_img)
    tilt, square, shadow_bent, shadow_half = collect(1, 4)
    omega = tilt / square
    rho_next = shadow_half - omega * shadow_bent
    beta = rho_next / rho * (alpha / omega)
    adj_ref[...] = alpha * b_ref[...] + omega * half[...]
    res_ref[...] = half[...] - omega * bent[...]
    direc[...] = res_ref[...] + beta * (b_ref[...] - omega * img[...])
    img2[...] = bent[...] + beta * (img[...] - omega * img2[...])
    receive(2, bent_img)
    img[...] = img2[...] - omega * bent_img[...]
    share(2, [(b_ref[...], img[...])])

    send_channels(3, img)
    local_part(3, img, img2)
    (shadow_image,) = collect(2, 1)
    alpha = rho_next / shadow_image
    half[...] = res_ref[...] - alpha * img[...]
    bent[...] = bent[...] - omega * bent_img[...]
    adj_ref[...] = adj_ref[...] + alpha * direc[...]
    receive(3, img2)
    bent[...] = bent[...] - alpha * img2[...]
    share(3, [(bent[...], half[...]), (bent[...], bent[...])])
    tilt, square = collect(3, 2)
    omega = tilt / square
    adj_ref[...] = adj_ref[...] + omega * half[...]
    res_ref[...] = half[...] - omega * bent[...]

    for step in range(4):
        for j in range(4):
            @pl.when(has_target(j))
            def _():
                message(step, j).wait_send()

        def sent(i, carry):
            partial_copy(step, lax.rem(me + i, n), me).wait_send()
            return carry

        lax.fori_loop(1, n, sent, 0)


def local(blocks, couplings, cotangent):
    tiles, slots, fields, _, cells = blocks.shape
    n = lax.axis_size("row")
    far = max(2, n // 8)
    field = (tiles, fields, cells)
    f32 = jnp.float32
    vmem = pl.BlockSpec(memory_space=pltpu.VMEM)
    return pl.pallas_call(
        functools.partial(kernel, n, far),
        out_shape=(jax.ShapeDtypeStruct(field, f32), jax.ShapeDtypeStruct(field, f32)),
        in_specs=[
            pl.BlockSpec(memory_space=pl.ANY),
            pl.BlockSpec(memory_space=pltpu.SMEM),
            vmem,
        ],
        out_specs=(vmem, vmem),
        scratch_shapes=[
            pltpu.VMEM((slots, tiles, fields, fields, cells), f32),
            pltpu.VMEM((2, fields, fields, cells), f32),
        ]
        + [pltpu.VMEM(field, f32)] * 6
        + [
            pltpu.VMEM((tiles + 1, fields, cells), f32),
            pltpu.VMEM((tiles + 1, fields, cells), f32),
            pltpu.VMEM((4, 4, tiles + 1, fields, cells), f32),
            pltpu.VMEM((4, 8, cells), f32),
            pltpu.VMEM((4, n, 8, cells), f32),
            pltpu.SemaphoreType.DMA((9,)),
            pltpu.SemaphoreType.DMA((4, 4)),
            pltpu.SemaphoreType.DMA((4, 4)),
            pltpu.SemaphoreType.DMA((4, n)),
            pltpu.SemaphoreType.DMA((4, n)),
        ]
        + [pltpu.VMEM((tiles + 1, fields, cells), f32)] * 16,
        compiler_params=pltpu.CompilerParams(
            collective_id=0, has_side_effects=True, vmem_limit_bytes=40 * 1024 * 1024
        ),
        name="adjoint_solve",
    )(blocks, couplings, cotangent)


def solution(mesh):
    placed = (
        P(("grp", "row"), None, None, None, None),
        P(("grp", "row"), None),
        P(("grp", "row"), None, None),
    )
    return jax.shard_map(
        local,
        mesh=mesh,
        in_specs=placed,
        out_specs=(P(("grp", "row"), None, None), P(("grp", "row"), None, None)),
        check_vma=False,
    )
```

```python
import functools

import jax
import jax.numpy as jnp
from jax import lax
from jax.experimental import pallas as pl
from jax.experimental.pallas import tpu as pltpu
from jax.sharding import PartitionSpec as P

MESH = pl.DeviceIdType.MESH
PAIRED = (1, 0, 3, 2)
ORDER = (2, 3, 0, 1)


def kernel(
    n, far, blocks_hbm, coup, b_ref, adj_ref, res_ref,
    blk, edge_blk, origin, img, img2, bent, bent_img, direc, half,
    send, recv, red_send, red,
    load_sem, send_sem, recv_sem, red_send_sem, red_recv_sem,
):
    fields, tiles, cells = b_ref.shape
    me = lax.axis_index("row")
    offsets = (1, -1, far, -far)
    body = fields * tiles

    def load(slot):
        return pltpu.make_async_copy(blocks_hbm.at[slot], blk.at[slot], load_sem.at[slot])

    edge_loads = (
        pltpu.make_async_copy(
            blocks_hbm.at[2, :, :, pl.ds(tiles - 8, 8)], edge_blk.at[0], load_sem.at[7]
        ),
        pltpu.make_async_copy(
            blocks_hbm.at[1, :, :, pl.ds(0, 8)], edge_blk.at[1], load_sem.at[8]
        ),
    )
    load(3 + ORDER[0]).start()
    load(3 + ORDER[1]).start()
    edge_loads[0].start()
    edge_loads[1].start()
    load(3 + ORDER[2]).start()
    load(3 + ORDER[3]).start()
    for slot in (1, 2, 0):
        load(slot).start()

    barrier = pltpu.get_barrier_semaphore()

    def greet(i, carry):
        other = lax.rem(me + i, n)
        pl.semaphore_signal(barrier, inc=1, device_id={"row": other}, device_id_type=MESH)
        return carry

    lax.fori_loop(1, n, greet, 0)

    def has_target(j):
        to = me + offsets[j]
        return jnp.logical_and(to >= 0, to < n)

    def has_source(j):
        start = me - offsets[j]
        return jnp.logical_and(start >= 0, start < n)

    for j in range(4):
        @pl.when(jnp.logical_not(has_source(j)))
        def _():
            for step in range(4):
                recv[step, j] = jnp.zeros(recv.shape[2:], jnp.float32)

    on_diagonal = lax.broadcasted_iota(jnp.int32, (tiles, tiles), 0) == (
        lax.broadcasted_iota(jnp.int32, (tiles, tiles), 1)
    )
    for j in range(4):
        row = jnp.bitwise_and(coup[PAIRED[j]:PAIRED[j] + 1, :], tiles - 1)
        spread = jnp.where(on_diagonal, jnp.broadcast_to(row, (tiles, tiles)), 0)
        column = jnp.sum(spread.astype(jnp.float32), axis=1, keepdims=True)
        origin[j] = jnp.broadcast_to(column.astype(jnp.int32), (tiles, cells))

    def message(step, j):
        rows = pl.ds(0, body + 8 if j < 2 else body)
        return pltpu.make_async_remote_copy(
            src_ref=send.at[step, j, rows],
            dst_ref=recv.at[step, j, rows],
            send_sem=send_sem.at[step, j],
            recv_sem=recv_sem.at[step, j],
            device_id={"row": me + offsets[j]},
            device_id_type=MESH,
        )

    lane = lax.broadcasted_iota(jnp.int32, (8, cells), 1)
    row8 = lax.broadcasted_iota(jnp.int32, (8, cells), 0)
    first_lane = lane == 0
    last_lane = lane == cells - 1

    def product(values, block):
        out = []
        for b in range(fields):
            total = block(0, b) * values[0]
            for a in range(1, fields):
                total = total + block(a, b) * values[a]
            out.append(total)
        return out

    def send_channels(step, field):
        for j in ORDER:
            if step == 0:
                load(3 + j).wait()

            @pl.loop(0, tiles // 8, unroll=True)
            def _(chunk):
                start = pl.multiple_of(chunk * 8, 8)
                rows = pl.ds(start, 8)
                values = [field[a, rows, :] for a in range(fields)]
                moved = product(values, lambda a, b: blk[3 + j, a, b, rows, :])
                for b in range(fields):
                    send[step, j, pl.ds(pl.multiple_of(b * tiles + start, 8), 8), :] = moved[b]

            if j < 2:
                if step == 0:
                    edge_loads[j].wait()
                rows = pl.ds(tiles - 8 if j == 0 else 0, 8)
                at = 7 if j == 0 else 0
                values = [field[a, rows, :] for a in range(fields)]
                moved = product(values, lambda a, b: edge_blk[j, a, b])
                edge = jnp.zeros((8, cells), jnp.float32)
                for b in range(fields):
                    shifted = moved[b] if b == at else pltpu.roll(moved[b], (b - at) % 8, 0)
                    edge = jnp.where(row8 == b, shifted, edge)
                send[step, j, pl.ds(body, 8), :] = pltpu.roll(edge, 1 if j == 0 else cells - 1, 1)
            if step == 0 and j == ORDER[0]:
                pl.semaphore_wait(barrier, n - 1)

            @pl.when(has_target(j))
            def _():
                message(step, j).start()

    def local_part(step, field, out):
        if step == 0:
            for slot in (1, 2, 0):
                load(slot).wait()
        chunks = tiles // 8
        values = [[field[a, pl.ds(8 * c, 8), :] for a in range(fields)] for c in range(chunks)]
        for b in range(fields):
            own, left, right = [], [], []
            for c in range(chunks):
                rows = pl.ds(8 * c, 8)
                sums = []
                for slot in range(3):
                    total = blk[slot, 0, b, rows, :] * values[c][0]
                    for a in range(1, fields):
                        total = total + blk[slot, a, b, rows, :] * values[c][a]
                    sums.append(total)
                own.append(sums[0])
                left.append(pltpu.roll(sums[1], cells - 1, 1))
                right.append(pltpu.roll(sums[2], 1, 1))
            up = [pltpu.roll(x, 7, 0) for x in left]
            down = [pltpu.roll(x, 1, 0) for x in right]
            for c in range(chunks):
                after = up[c + 1] if c + 1 < chunks else jnp.zeros((8, cells), jnp.float32)
                before = down[c - 1] if c else jnp.zeros((8, cells), jnp.float32)
                after = jnp.where(row8 == 7, after, up[c])
                before = jnp.where(row8 == 0, before, down[c])
                out[b, pl.ds(8 * c, 8), :] = (
                    own[c]
                    + jnp.where(last_lane, after, left[c])
                    + jnp.where(first_lane, before, right[c])
                )

    def receive(step, out):
        chunks = tiles // 8
        for j in ORDER:
            @pl.when(has_source(j))
            def _():
                message(step, j).wait_recv()

            @pl.loop(0, fields, unroll=True)
            def _(b):
                parts = [
                    recv[step, j, pl.ds(pl.multiple_of(b * tiles + 8 * c, 8), 8), :]
                    for c in range(chunks)
                ]
                for c in range(chunks):
                    place = origin[j, pl.ds(8 * c, 8), :]
                    low = jnp.bitwise_and(place, 7)
                    high = jnp.right_shift(place, 3)
                    total = jnp.take_along_axis(parts[0], low, axis=0)
                    for k in range(1, chunks):
                        total = jnp.where(
                            high == k, jnp.take_along_axis(parts[k], low, axis=0), total
                        )
                    out[b, pl.ds(8 * c, 8), :] = out[b, pl.ds(8 * c, 8), :] + total

            if j < 2:
                edge = recv[step, j, pl.ds(body, 8), :]
                at = 0 if j == 0 else 7
                rows = pl.ds(0 if j == 0 else tiles - 8, 8)
                corner = jnp.logical_and(row8 == at, first_lane if j == 0 else last_lane)
                for b in range(fields):
                    shifted = edge if b == at else pltpu.roll(edge, (at - b) % 8, 0)
                    out[b, rows, :] = out[b, rows, :] + jnp.where(corner, shifted, 0.0)

    def partial_copy(step, other, origin):
        return pltpu.make_async_remote_copy(
            src_ref=red_send.at[step],
            dst_ref=red.at[step, origin],
            send_sem=red_send_sem.at[step, other],
            recv_sem=red_recv_sem.at[step, origin],
            device_id={"row": other},
            device_id_type=MESH,
        )

    def share(step, pairs):
        rows = [
            jnp.sum(jnp.sum(x * y, axis=0), axis=0, keepdims=True) for x, y in pairs
        ]
        rows += [jnp.zeros((8 - len(rows), cells), jnp.float32)]
        tile = jnp.concatenate(rows, axis=0)
        red_send[step] = tile
        red[step, me] = tile

        def go(i, carry):
            partial_copy(step, lax.rem(me + i, n), me).start()
            return carry

        lax.fori_loop(1, n, go, 0)

    def collect(step, count):
        def arrive(i, carry):
            other = lax.rem(me + i, n)
            partial_copy(step, other, other).wait_recv()
            return carry

        lax.fori_loop(1, n, arrive, 0)
        total = jnp.sum(jnp.sum(red[step], axis=0), axis=1, keepdims=True)
        return [total[q:q + 1] for q in range(count)]

    send_channels(0, b_ref)
    local_part(0, b_ref, img)
    receive(0, img)
    b = b_ref[...]
    share(0, [(b, b), (b, img[...])])

    send_channels(1, img)
    local_part(1, img, img2)
    rho, shadow_image = collect(0, 2)
    alpha = rho / shadow_image
    receive(1, img2)
    half[...] = b_ref[...] - alpha * img[...]
    bent[...] = img[...] - alpha * img2[...]
    share(1, [
        (bent[...], half[...]), (bent[...], bent[...]),
        (b_ref[...], bent[...]), (b_ref[...], half[...]),
    ])

    send_channels(2, bent)
    local_part(2, bent, bent_img)
    tilt, square, shadow_bent, shadow_half = collect(1, 4)
    omega = tilt / square
    rho_next = shadow_half - omega * shadow_bent
    beta = rho_next / rho * (alpha / omega)
    adj_ref[...] = alpha * b_ref[...] + omega * half[...]
    res_ref[...] = half[...] - omega * bent[...]
    direc[...] = res_ref[...] + beta * (b_ref[...] - omega * img[...])
    img2[...] = bent[...] + beta * (img[...] - omega * img2[...])
    receive(2, bent_img)
    img[...] = img2[...] - omega * bent_img[...]
    share(2, [(b_ref[...], img[...])])

    send_channels(3, img)
    local_part(3, img, img2)
    (shadow_image,) = collect(2, 1)
    alpha = rho_next / shadow_image
    half[...] = res_ref[...] - alpha * img[...]
    bent[...] = bent[...] - omega * bent_img[...]
    adj_ref[...] = adj_ref[...] + alpha * direc[...]
    receive(3, img2)
    bent[...] = bent[...] - alpha * img2[...]
    share(3, [(bent[...], half[...]), (bent[...], bent[...])])
    tilt, square = collect(3, 2)
    omega = tilt / square
    adj_ref[...] = adj_ref[...] + omega * half[...]
    res_ref[...] = half[...] - omega * bent[...]

    for step in range(4):
        for j in range(4):
            @pl.when(has_target(j))
            def _():
                message(step, j).wait_send()

        def sent(i, carry):
            partial_copy(step, lax.rem(me + i, n), me).wait_send()
            return carry

        lax.fori_loop(1, n, sent, 0)


def local(blocks, couplings, cotangent):
    tiles, slots, fields, _, cells = blocks.shape
    n = lax.axis_size("row")
    far = max(2, n // 8)
    field = (fields, tiles, cells)
    f32 = jnp.float32
    vmem = pl.BlockSpec(memory_space=pltpu.VMEM)
    adjoint, residual = pl.pallas_call(
        functools.partial(kernel, n, far),
        out_shape=(jax.ShapeDtypeStruct(field, f32), jax.ShapeDtypeStruct(field, f32)),
        in_specs=[pl.BlockSpec(memory_space=pl.ANY), vmem, vmem],
        out_specs=(vmem, vmem),
        scratch_shapes=[
            pltpu.VMEM((slots, fields, fields, tiles, cells), f32),
            pltpu.VMEM((2, fields, fields, 8, cells), f32),
            pltpu.VMEM((4, tiles, cells), jnp.int32),
        ]
        + [pltpu.VMEM(field, f32)] * 6
        + [
            pltpu.VMEM((4, 4, fields * tiles + 8, cells), f32),
            pltpu.VMEM((4, 4, fields * tiles + 8, cells), f32),
            pltpu.VMEM((4, 8, cells), f32),
            pltpu.VMEM((4, n, 8, cells), f32),
            pltpu.SemaphoreType.DMA((9,)),
            pltpu.SemaphoreType.DMA((4, 4)),
            pltpu.SemaphoreType.DMA((4, 4)),
            pltpu.SemaphoreType.DMA((4, n)),
            pltpu.SemaphoreType.DMA((4, n)),
        ],
        compiler_params=pltpu.CompilerParams(
            collective_id=0, has_side_effects=True, vmem_limit_bytes=40 * 1024 * 1024
        ),
        name="adjoint_solve",
    )(
        jnp.transpose(blocks, (1, 2, 3, 0, 4)),
        jnp.transpose(couplings),
        jnp.transpose(cotangent, (1, 0, 2)),
    )
    return jnp.transpose(adjoint, (1, 0, 2)), jnp.transpose(residual, (1, 0, 2))


def solution(mesh):
    placed = (
        P(("grp", "row"), None, None, None, None),
        P(("grp", "row"), None),
        P(("grp", "row"), None, None),
    )
    return jax.shard_map(
        local,
        mesh=mesh,
        in_specs=placed,
        out_specs=(P(("grp", "row"), None, None), P(("grp", "row"), None, None)),
        check_vma=False,
    )
```

```python
import functools

import jax
import jax.numpy as jnp
from jax import lax
from jax.experimental import pallas as pl
from jax.experimental.pallas import tpu as pltpu
from jax.sharding import PartitionSpec as P

MESH = pl.DeviceIdType.MESH
PAIRED = (1, 0, 3, 2)
SUMS = (2, 4, 1, 2)
ORDER = (2, 3, 0, 1)


def kernel(
    n, far, blocks_hbm, coup, b_ref, adj_ref, res_ref,
    blk, edge_blk, origin, img, img2, bent, bent_img, direc, half,
    send, recv, load_sem, send_sem, recv_sem, red_send_sem, red_recv_sem, *sums
):
    red_send, red = sums[:4], sums[4:]
    fields, tiles, cells = b_ref.shape
    me = lax.axis_index("row")
    offsets = (1, -1, far, -far)
    body = fields * tiles
    paired = far == 2 and n % 2 == 0

    def load(slot):
        return pltpu.make_async_copy(blocks_hbm.at[slot], blk.at[slot], load_sem.at[slot])

    edge_loads = (
        pltpu.make_async_copy(
            blocks_hbm.at[2, :, :, pl.ds(tiles - 8, 8)], edge_blk.at[0], load_sem.at[7]
        ),
        pltpu.make_async_copy(
            blocks_hbm.at[1, :, :, pl.ds(0, 8)], edge_blk.at[1], load_sem.at[8]
        ),
    )
    parity = lax.rem(me, 2)
    order = (2 + parity, 3 - parity, 1 - parity, parity) if paired else ORDER
    load(3 + order[0]).start()
    load(3 + order[1]).start()
    edge_loads[0].start()
    edge_loads[1].start()
    load(3 + order[2]).start()
    load(3 + order[3]).start()
    for slot in (1, 2, 0):
        load(slot).start()

    barrier = pltpu.get_barrier_semaphore()

    def greet(i, carry):
        other = lax.rem(me + i, n)
        pl.semaphore_signal(barrier, inc=1, device_id={"row": other}, device_id_type=MESH)
        return carry

    lax.fori_loop(1, n, greet, 0)

    def has_target(j):
        to = me + offsets[j]
        return jnp.logical_and(to >= 0, to < n)

    def has_source(j):
        start = me - offsets[j]
        return jnp.logical_and(start >= 0, start < n)

    def clear(kind):
        for step in range(4):
            recv[step, kind] = jnp.zeros(recv.shape[2:], jnp.float32)

    if paired:
        at_end = lax.rem(me, 2) == 0
        sign0 = jnp.where(at_end, -1, 1)
        no_outward = jnp.logical_or(me + sign0 < 0, me + sign0 >= n)
        no_inward = jnp.logical_or(me - 2 * sign0 < 0, me - 2 * sign0 >= n)
        pl.when(no_outward)(lambda: clear(3))
        pl.when(no_inward)(lambda: clear(1))
    else:
        for j in range(4):
            pl.when(jnp.logical_not(has_source(j)))(functools.partial(clear, j))

    down = lax.broadcasted_iota(jnp.int32, (tiles, tiles), 0)
    across = lax.broadcasted_iota(jnp.int32, (tiles, tiles), 1)

    def column_of(row, inverse):
        row = jnp.broadcast_to(jnp.bitwise_and(row, tiles - 1), (tiles, tiles))
        spread = jnp.where(row == down, across, 0) if inverse else jnp.where(down == across, row, 0)
        column = jnp.sum(spread.astype(jnp.float32), axis=1, keepdims=True)
        return jnp.broadcast_to(column.astype(jnp.int32), (tiles, cells))

    if paired:
        even = lax.rem(me, 2) == 0
        pair_rows = [jnp.where(even, coup[k:k + 1, :], coup[m:m + 1, :]) for k, m in ((0, 1), (2, 3), (1, 0))]
        origin[0] = column_of(pair_rows[0], False)
        origin[1] = column_of(pair_rows[1], False)
        origin[2] = column_of(pair_rows[1], True)
        origin[3] = column_of(pair_rows[2], True)
    else:
        for j in range(4):
            origin[j] = column_of(coup[PAIRED[j]:PAIRED[j] + 1, :], False)

    def message(step, j):
        rows = pl.ds(0, body + 8 if j < 2 else body)
        return pltpu.make_async_remote_copy(
            src_ref=send.at[step, j, rows],
            dst_ref=recv.at[step, j, rows],
            send_sem=send_sem.at[step, j],
            recv_sem=recv_sem.at[step, j],
            device_id={"row": me + offsets[j]},
            device_id_type=MESH,
        )

    lane = lax.broadcasted_iota(jnp.int32, (8, cells), 1)
    row8 = lax.broadcasted_iota(jnp.int32, (8, cells), 0)
    first_lane = lane == 0
    last_lane = lane == cells - 1

    def product(values, block):
        out = []
        for b in range(fields):
            total = block(0, b) * values[0]
            for a in range(1, fields):
                total = total + block(a, b) * values[a]
            out.append(total)
        return out

    def send_channels(step, field):
        for j in ORDER:
            if step == 0:
                load(3 + j).wait()

            @pl.loop(0, tiles // 8, unroll=True)
            def _(chunk):
                start = pl.multiple_of(chunk * 8, 8)
                rows = pl.ds(start, 8)
                values = [field[a, rows, :] for a in range(fields)]
                moved = product(values, lambda a, b: blk[3 + j, a, b, rows, :])
                for b in range(fields):
                    send[step, j, pl.ds(pl.multiple_of(b * tiles + start, 8), 8), :] = moved[b]

            if j < 2:
                if step == 0:
                    edge_loads[j].wait()
                rows = pl.ds(tiles - 8 if j == 0 else 0, 8)
                at = 7 if j == 0 else 0
                values = [field[a, rows, :] for a in range(fields)]
                moved = product(values, lambda a, b: edge_blk[j, a, b])
                edge = jnp.zeros((8, cells), jnp.float32)
                for b in range(fields):
                    shifted = moved[b] if b == at else pltpu.roll(moved[b], (b - at) % 8, 0)
                    edge = jnp.where(row8 == b, shifted, edge)
                send[step, j, pl.ds(body, 8), :] = pltpu.roll(edge, 1 if j == 0 else cells - 1, 1)
            if step == 0 and j == ORDER[0]:
                pl.semaphore_wait(barrier, n - 1)

            @pl.when(has_target(j))
            def _():
                message(step, j).start()

    def local_part(step, field, out):
        if step == 0:
            for slot in (1, 2, 0):
                load(slot).wait()
        chunks = tiles // 8
        values = [[field[a, pl.ds(8 * c, 8), :] for a in range(fields)] for c in range(chunks)]
        for b in range(fields):
            own, left, right = [], [], []
            for c in range(chunks):
                rows = pl.ds(8 * c, 8)
                sums = []
                for slot in range(3):
                    total = blk[slot, 0, b, rows, :] * values[c][0]
                    for a in range(1, fields):
                        total = total + blk[slot, a, b, rows, :] * values[c][a]
                    sums.append(total)
                own.append(sums[0])
                left.append(pltpu.roll(sums[1], cells - 1, 1))
                right.append(pltpu.roll(sums[2], 1, 1))
            up = [pltpu.roll(x, 7, 0) for x in left]
            down = [pltpu.roll(x, 1, 0) for x in right]
            for c in range(chunks):
                after = up[c + 1] if c + 1 < chunks else jnp.zeros((8, cells), jnp.float32)
                before = down[c - 1] if c else jnp.zeros((8, cells), jnp.float32)
                after = jnp.where(row8 == 7, after, up[c])
                before = jnp.where(row8 == 0, before, down[c])
                out[b, pl.ds(8 * c, 8), :] = (
                    own[c]
                    + jnp.where(last_lane, after, left[c])
                    + jnp.where(first_lane, before, right[c])
                )

    def receive(step, out):
        chunks = tiles // 8
        for j in ORDER:
            @pl.when(has_source(j))
            def _():
                message(step, j).wait_recv()

            @pl.loop(0, fields, unroll=True)
            def _(b):
                parts = [
                    recv[step, j, pl.ds(pl.multiple_of(b * tiles + 8 * c, 8), 8), :]
                    for c in range(chunks)
                ]
                for c in range(chunks):
                    place = origin[j, pl.ds(8 * c, 8), :]
                    low = jnp.bitwise_and(place, 7)
                    high = jnp.right_shift(place, 3)
                    total = jnp.take_along_axis(parts[0], low, axis=0)
                    for k in range(1, chunks):
                        total = jnp.where(
                            high == k, jnp.take_along_axis(parts[k], low, axis=0), total
                        )
                    out[b, pl.ds(8 * c, 8), :] = out[b, pl.ds(8 * c, 8), :] + total

            if j < 2:
                edge = recv[step, j, pl.ds(body, 8), :]
                at = 0 if j == 0 else 7
                rows = pl.ds(0 if j == 0 else tiles - 8, 8)
                corner = jnp.logical_and(row8 == at, first_lane if j == 0 else last_lane)
                for b in range(fields):
                    shifted = edge if b == at else pltpu.roll(edge, (at - b) % 8, 0)
                    out[b, rows, :] = out[b, rows, :] + jnp.where(corner, shifted, 0.0)

    core = lax.rem(me, 2)
    sign = 2 * core - 1
    outward = jnp.logical_and(me + sign >= 0, me + sign < n)
    inward = jnp.logical_and(me - 2 * sign >= 0, me - 2 * sign < n)
    NEAR, SOLO, RELAY, MERGED = range(4)
    reach = (-sign, 2 * sign, -sign, sign)
    channel = (core, 3 - core, 2 + core, 1 - core)

    def pair_message(step, kind):
        rows = pl.ds(0, body + 8 if kind in (NEAR, MERGED) else body)
        return pltpu.make_async_remote_copy(
            src_ref=send.at[step, kind, rows],
            dst_ref=recv.at[step, kind, rows],
            send_sem=send_sem.at[step, kind],
            recv_sem=recv_sem.at[step, kind],
            device_id={"row": me + reach[kind]},
            device_id_type=MESH,
        )

    def permuted(parts, which):
        out = []
        for c in range(len(parts)):
            place = origin[which, pl.ds(8 * c, 8), :]
            low = jnp.bitwise_and(place, 7)
            high = jnp.right_shift(place, 3)
            total = jnp.take_along_axis(parts[0], low, axis=0)
            for k in range(1, len(parts)):
                total = jnp.where(high == k, jnp.take_along_axis(parts[k], low, axis=0), total)
            out.append(total)
        return out

    def fill(step, field, kind):
        chunks = tiles // 8
        slot = 3 + channel[kind]
        for b in range(fields):
            parts = []
            for c in range(chunks):
                rows = pl.ds(8 * c, 8)
                total = blk[slot, 0, b, rows, :] * field[0, rows, :]
                for a in range(1, fields):
                    total = total + blk[slot, a, b, rows, :] * field[a, rows, :]
                parts.append(total)
            if kind in (RELAY, MERGED):
                parts = permuted(parts, kind)
            for c in range(chunks):
                send[step, kind, pl.ds(b * tiles + 8 * c, 8), :] = parts[c]

    def edge_row(field, which):
        rows = pl.ds(tiles - 8 if which == 0 else 0, 8)
        at = 7 if which == 0 else 0
        values = [field[a, rows, :] for a in range(fields)]
        moved = product(values, lambda a, b: edge_blk[which, a, b])
        edge = jnp.zeros((8, cells), jnp.float32)
        for b in range(fields):
            shifted = moved[b] if b == at else pltpu.roll(moved[b], (b - at) % 8, 0)
            edge = jnp.where(row8 == b, shifted, edge)
        return pltpu.roll(edge, 1 if which == 0 else cells - 1, 1)

    def send_first(step, field):
        if step == 0:
            load(3 + channel[RELAY]).wait()
        fill(step, field, RELAY)
        if step == 0:
            pl.semaphore_wait(barrier, n - 1)

        @pl.when(inward)
        def _():
            pair_message(step, RELAY).start()

        if step == 0:
            load(3 + channel[SOLO]).wait()
        fill(step, field, SOLO)

        @pl.when(outward)
        def _():
            pair_message(step, SOLO).start()

        if step == 0:
            for which in range(2):
                edge_loads[which].wait()
        ahead, behind = edge_row(field, 0), edge_row(field, 1)
        first = core == 0
        send[step, NEAR, pl.ds(body, 8), :] = jnp.where(first, ahead, behind)
        send[step, MERGED, pl.ds(body, 8), :] = jnp.where(first, behind, ahead)
        if step == 0:
            load(3 + channel[MERGED]).wait()
        fill(step, field, MERGED)
        if step == 0:
            load(3 + channel[NEAR]).wait()
        fill(step, field, NEAR)
        pair_message(step, NEAR).start()

        @pl.when(outward)
        def _():
            pair_message(step, RELAY).wait_recv()
            send[step, MERGED, pl.ds(0, body), :] = (
                send[step, MERGED, pl.ds(0, body), :] + recv[step, RELAY, pl.ds(0, body), :]
            )
            pair_message(step, MERGED).start()

    def pair_receive(step, out):
        chunks = tiles // 8
        for kind in (NEAR, SOLO, MERGED):
            if kind == NEAR:
                pair_message(step, kind).wait_recv()
            else:
                @pl.when(inward if kind == SOLO else outward)
                def _():
                    pair_message(step, kind).wait_recv()

            for b in range(fields):
                parts = [
                    recv[step, kind, pl.ds(b * tiles + 8 * c, 8), :] for c in range(chunks)
                ]
                if kind != MERGED:
                    parts = permuted(parts, kind)
                for c in range(chunks):
                    rows = pl.ds(8 * c, 8)
                    out[b, rows, :] = out[b, rows, :] + parts[c]
        near, merged = recv[step, NEAR, pl.ds(body, 8), :], recv[step, MERGED, pl.ds(body, 8), :]
        first = core == 0
        for j in range(2):
            edge = jnp.where(first, merged, near) if j == 0 else jnp.where(first, near, merged)
            at = 0 if j == 0 else 7
            rows = pl.ds(0 if j == 0 else tiles - 8, 8)
            corner = jnp.logical_and(row8 == at, first_lane if j == 0 else last_lane)
            for b in range(fields):
                shifted = edge if b == at else pltpu.roll(edge, (at - b) % 8, 0)
                out[b, rows, :] = out[b, rows, :] + jnp.where(corner, shifted, 0.0)

    if paired:
        send_channels, receive = send_first, pair_receive

    def partial_copy(step, other, source):
        return pltpu.make_async_remote_copy(
            src_ref=red_send[step],
            dst_ref=red[step].at[source],
            send_sem=red_send_sem.at[step, other],
            recv_sem=red_recv_sem.at[step, source],
            device_id={"row": other},
            device_id_type=MESH,
        )

    def share(step, pairs):
        rows = [
            jnp.sum(jnp.sum(x * y, axis=0), axis=0, keepdims=True) for x, y in pairs
        ]
        row = jnp.concatenate(rows, axis=0)
        red_send[step][...] = row
        red[step][me] = row

        def go(i, carry):
            partial_copy(step, lax.rem(me + i, n), me).start()
            return carry

        lax.fori_loop(1, n, go, 0, unroll=True)

    def collect(step, count):
        def arrive(i, carry):
            other = lax.rem(me + i, n)
            partial_copy(step, other, other).wait_recv()
            return carry

        lax.fori_loop(1, n, arrive, 0, unroll=True)
        total = jnp.sum(jnp.sum(red[step][...], axis=0), axis=1, keepdims=True)
        return [total[q:q + 1] for q in range(count)]

    send_channels(0, b_ref)
    local_part(0, b_ref, img)
    receive(0, img)
    b = b_ref[...]
    share(0, [(b, b), (b, img[...])])

    send_channels(1, img)
    local_part(1, img, img2)
    rho, shadow_image = collect(0, 2)
    alpha = rho / shadow_image
    receive(1, img2)
    half[...] = b_ref[...] - alpha * img[...]
    bent[...] = img[...] - alpha * img2[...]
    share(1, [
        (bent[...], half[...]), (bent[...], bent[...]),
        (b_ref[...], bent[...]), (b_ref[...], half[...]),
    ])

    send_channels(2, bent)
    local_part(2, bent, bent_img)
    tilt, square, shadow_bent, shadow_half = collect(1, 4)
    omega = tilt / square
    rho_next = shadow_half - omega * shadow_bent
    beta = rho_next / rho * (alpha / omega)
    adj_ref[...] = alpha * b_ref[...] + omega * half[...]
    res_ref[...] = half[...] - omega * bent[...]
    direc[...] = res_ref[...] + beta * (b_ref[...] - omega * img[...])
    img2[...] = bent[...] + beta * (img[...] - omega * img2[...])
    receive(2, bent_img)
    img[...] = img2[...] - omega * bent_img[...]
    share(2, [(b_ref[...], img[...])])

    send_channels(3, img)
    local_part(3, img, img2)
    (shadow_image,) = collect(2, 1)
    alpha = rho_next / shadow_image
    half[...] = res_ref[...] - alpha * img[...]
    bent[...] = bent[...] - omega * bent_img[...]
    adj_ref[...] = adj_ref[...] + alpha * direc[...]
    receive(3, img2)
    bent[...] = bent[...] - alpha * img2[...]
    share(3, [(bent[...], half[...]), (bent[...], bent[...])])
    tilt, square = collect(3, 2)
    omega = tilt / square
    adj_ref[...] = adj_ref[...] + omega * half[...]
    res_ref[...] = half[...] - omega * bent[...]

    for step in range(4):
        if paired:
            pair_message(step, NEAR).wait_send()

            @pl.when(inward)
            def _():
                pair_message(step, RELAY).wait_send()

            @pl.when(outward)
            def _():
                pair_message(step, SOLO).wait_send()
                pair_message(step, MERGED).wait_send()
        else:
            for j in range(4):
                @pl.when(has_target(j))
                def _():
                    message(step, j).wait_send()

        def sent(i, carry):
            partial_copy(step, lax.rem(me + i, n), me).wait_send()
            return carry

        lax.fori_loop(1, n, sent, 0)


def local(blocks, couplings, cotangent):
    tiles, slots, fields, _, cells = blocks.shape
    n = lax.axis_size("row")
    far = max(2, n // 8)
    field = (fields, tiles, cells)
    f32 = jnp.float32
    vmem = pl.BlockSpec(memory_space=pltpu.VMEM)
    adjoint, residual = pl.pallas_call(
        functools.partial(kernel, n, far),
        out_shape=(jax.ShapeDtypeStruct(field, f32), jax.ShapeDtypeStruct(field, f32)),
        in_specs=[pl.BlockSpec(memory_space=pltpu.HBM), vmem, vmem],
        out_specs=(vmem, vmem),
        scratch_shapes=[
            pltpu.VMEM((slots, fields, fields, tiles, cells), f32),
            pltpu.VMEM((2, fields, fields, 8, cells), f32),
            pltpu.VMEM((4, tiles, cells), jnp.int32),
        ]
        + [pltpu.VMEM(field, f32)] * 6
        + [
            pltpu.VMEM((4, 4, fields * tiles + 8, cells), f32),
            pltpu.VMEM((4, 4, fields * tiles + 8, cells), f32),
            pltpu.SemaphoreType.DMA((9,)),
            pltpu.SemaphoreType.DMA((4, 4)),
            pltpu.SemaphoreType.DMA((4, 4)),
            pltpu.SemaphoreType.DMA((4, n)),
            pltpu.SemaphoreType.DMA((4, n)),
        ]
        + [pltpu.VMEM((count, cells), f32) for count in SUMS]
        + [pltpu.VMEM((n, count, cells), f32) for count in SUMS],
        compiler_params=pltpu.CompilerParams(
            collective_id=0, has_side_effects=True, vmem_limit_bytes=60 * 1024 * 1024
        ),
        name="adjoint_solve",
    )(
        jnp.transpose(blocks, (1, 2, 3, 0, 4)),
        jnp.transpose(couplings),
        jnp.transpose(cotangent, (1, 0, 2)),
    )
    return jnp.transpose(adjoint, (1, 0, 2)), jnp.transpose(residual, (1, 0, 2))


def solution(mesh):
    placed = (
        P(("grp", "row"), None, None, None, None),
        P(("grp", "row"), None),
        P(("grp", "row"), None, None),
    )
    return jax.shard_map(
        local,
        mesh=mesh,
        in_specs=placed,
        out_specs=(P(("grp", "row"), None, None), P(("grp", "row"), None, None)),
        check_vma=False,
    )
```

```python
import functools

import jax
import jax.numpy as jnp
from jax import lax
from jax.experimental import pallas as pl
from jax.experimental.pallas import tpu as pltpu
from jax.sharding import PartitionSpec as P

MESH = pl.DeviceIdType.MESH
PAIRED = (1, 0, 3, 2)
SUMS = (2, 4, 1, 2)
ORDER = (2, 3, 0, 1)


def kernel(
    n, far, group, blocks_hbm, coup_hbm, b_hbm, adj_ref, res_ref,
    coup, b_ref,
    blk, edge_blk, origin, img, img2, bent, bent_img, direc, half,
    send, recv, load_sem, send_sem, recv_sem,
    first_send_sem, first_recv_sem, second_send_sem, second_recv_sem, *sums
):
    first_sems = (first_send_sem, first_recv_sem)
    second_sems = (second_send_sem, second_recv_sem)
    fields, tiles, cells = b_ref.shape
    me = lax.axis_index("row")
    offsets = (1, -1, far, -far)
    body = fields * tiles
    paired = far == 2 and n % 2 == 0

    def load(slot):
        return pltpu.make_async_copy(blocks_hbm.at[slot], blk.at[slot], load_sem.at[slot])

    edge_loads = (
        pltpu.make_async_copy(
            blocks_hbm.at[2, :, :, pl.ds(tiles - 8, 8)], edge_blk.at[0], load_sem.at[7]
        ),
        pltpu.make_async_copy(
            blocks_hbm.at[1, :, :, pl.ds(0, 8)], edge_blk.at[1], load_sem.at[8]
        ),
    )
    b_load = pltpu.make_async_copy(b_hbm, b_ref, load_sem.at[9])
    coup_load = pltpu.make_async_copy(coup_hbm, coup, load_sem.at[10])
    coup_load.start()
    b_load.start()
    parity = lax.rem(me, 2)
    order = (2 + parity, 3 - parity, 1 - parity, parity) if paired else ORDER
    load(3 + order[0]).start()
    load(3 + order[1]).start()
    edge_loads[0].start()
    edge_loads[1].start()
    load(3 + order[2]).start()
    load(3 + order[3]).start()
    for slot in (1, 2, 0):
        load(slot).start()

    barrier = pltpu.get_barrier_semaphore()

    def greet(i, carry):
        other = lax.rem(me + i, n)
        pl.semaphore_signal(barrier, inc=1, device_id={"row": other}, device_id_type=MESH)
        return carry

    lax.fori_loop(1, n, greet, 0)

    def has_target(j):
        to = me + offsets[j]
        return jnp.logical_and(to >= 0, to < n)

    def has_source(j):
        start = me - offsets[j]
        return jnp.logical_and(start >= 0, start < n)

    def clear(kind):
        for step in range(4):
            recv[step, kind] = jnp.zeros(recv.shape[2:], jnp.float32)

    if paired:
        at_end = lax.rem(me, 2) == 0
        sign0 = jnp.where(at_end, -1, 1)
        no_outward = jnp.logical_or(me + sign0 < 0, me + sign0 >= n)
        no_inward = jnp.logical_or(me - 2 * sign0 < 0, me - 2 * sign0 >= n)
        pl.when(no_outward)(lambda: clear(3))
        pl.when(no_inward)(lambda: clear(1))
    else:
        for j in range(4):
            pl.when(jnp.logical_not(has_source(j)))(functools.partial(clear, j))

    down = lax.broadcasted_iota(jnp.int32, (tiles, tiles), 0)
    across = lax.broadcasted_iota(jnp.int32, (tiles, tiles), 1)

    def column_of(row, inverse):
        row = jnp.broadcast_to(jnp.bitwise_and(row, tiles - 1), (tiles, tiles))
        spread = jnp.where(row == down, across, 0) if inverse else jnp.where(down == across, row, 0)
        column = jnp.sum(spread.astype(jnp.float32), axis=1, keepdims=True)
        return jnp.broadcast_to(column.astype(jnp.int32), (tiles, cells))

    coup_load.wait()
    if paired:
        even = lax.rem(me, 2) == 0
        pair_rows = [jnp.where(even, coup[k:k + 1, :], coup[m:m + 1, :]) for k, m in ((0, 1), (2, 3), (1, 0))]
        origin[0] = column_of(pair_rows[0], False)
        origin[1] = column_of(pair_rows[1], False)
        origin[2] = column_of(pair_rows[1], True)
        origin[3] = column_of(pair_rows[2], True)
    else:
        for j in range(4):
            origin[j] = column_of(coup[PAIRED[j]:PAIRED[j] + 1, :], False)

    def message(step, j):
        rows = pl.ds(0, body + 8 if j < 2 else body)
        return pltpu.make_async_remote_copy(
            src_ref=send.at[step, j, rows],
            dst_ref=recv.at[step, j, rows],
            send_sem=send_sem.at[step, j],
            recv_sem=recv_sem.at[step, j],
            device_id={"row": me + offsets[j]},
            device_id_type=MESH,
        )

    lane = lax.broadcasted_iota(jnp.int32, (8, cells), 1)
    row8 = lax.broadcasted_iota(jnp.int32, (8, cells), 0)
    first_lane = lane == 0
    last_lane = lane == cells - 1

    def product(values, block):
        out = []
        for b in range(fields):
            total = block(0, b) * values[0]
            for a in range(1, fields):
                total = total + block(a, b) * values[a]
            out.append(total)
        return out

    def send_channels(step, field):
        for j in ORDER:
            if step == 0:
                load(3 + j).wait()

            @pl.loop(0, tiles // 8, unroll=True)
            def _(chunk):
                start = pl.multiple_of(chunk * 8, 8)
                rows = pl.ds(start, 8)
                values = [field[a, rows, :] for a in range(fields)]
                moved = product(values, lambda a, b: blk[3 + j, a, b, rows, :])
                for b in range(fields):
                    send[step, j, pl.ds(pl.multiple_of(b * tiles + start, 8), 8), :] = moved[b]

            if j < 2:
                if step == 0:
                    edge_loads[j].wait()
                rows = pl.ds(tiles - 8 if j == 0 else 0, 8)
                at = 7 if j == 0 else 0
                values = [field[a, rows, :] for a in range(fields)]
                moved = product(values, lambda a, b: edge_blk[j, a, b])
                edge = jnp.zeros((8, cells), jnp.float32)
                for b in range(fields):
                    shifted = moved[b] if b == at else pltpu.roll(moved[b], (b - at) % 8, 0)
                    edge = jnp.where(row8 == b, shifted, edge)
                send[step, j, pl.ds(body, 8), :] = pltpu.roll(edge, 1 if j == 0 else cells - 1, 1)
            if step == 0 and j == ORDER[0]:
                pl.semaphore_wait(barrier, n - 1)

            @pl.when(has_target(j))
            def _():
                message(step, j).start()

    def local_part(step, field, out):
        if step == 0:
            for slot in (1, 2, 0):
                load(slot).wait()
        chunks = tiles // 8
        values = [[field[a, pl.ds(8 * c, 8), :] for a in range(fields)] for c in range(chunks)]
        for b in range(fields):
            own, left, right = [], [], []
            for c in range(chunks):
                rows = pl.ds(8 * c, 8)
                sums = []
                for slot in range(3):
                    total = blk[slot, 0, b, rows, :] * values[c][0]
                    for a in range(1, fields):
                        total = total + blk[slot, a, b, rows, :] * values[c][a]
                    sums.append(total)
                own.append(sums[0])
                left.append(pltpu.roll(sums[1], cells - 1, 1))
                right.append(pltpu.roll(sums[2], 1, 1))
            up = [pltpu.roll(x, 7, 0) for x in left]
            down = [pltpu.roll(x, 1, 0) for x in right]
            for c in range(chunks):
                after = up[c + 1] if c + 1 < chunks else jnp.zeros((8, cells), jnp.float32)
                before = down[c - 1] if c else jnp.zeros((8, cells), jnp.float32)
                after = jnp.where(row8 == 7, after, up[c])
                before = jnp.where(row8 == 0, before, down[c])
                out[b, pl.ds(8 * c, 8), :] = (
                    own[c]
                    + jnp.where(last_lane, after, left[c])
                    + jnp.where(first_lane, before, right[c])
                )

    def receive(step, out):
        chunks = tiles // 8
        for j in ORDER:
            @pl.when(has_source(j))
            def _():
                message(step, j).wait_recv()

            @pl.loop(0, fields, unroll=True)
            def _(b):
                parts = [
                    recv[step, j, pl.ds(pl.multiple_of(b * tiles + 8 * c, 8), 8), :]
                    for c in range(chunks)
                ]
                for c in range(chunks):
                    place = origin[j, pl.ds(8 * c, 8), :]
                    low = jnp.bitwise_and(place, 7)
                    high = jnp.right_shift(place, 3)
                    total = jnp.take_along_axis(parts[0], low, axis=0)
                    for k in range(1, chunks):
                        total = jnp.where(
                            high == k, jnp.take_along_axis(parts[k], low, axis=0), total
                        )
                    out[b, pl.ds(8 * c, 8), :] = out[b, pl.ds(8 * c, 8), :] + total

            if j < 2:
                edge = recv[step, j, pl.ds(body, 8), :]
                at = 0 if j == 0 else 7
                rows = pl.ds(0 if j == 0 else tiles - 8, 8)
                corner = jnp.logical_and(row8 == at, first_lane if j == 0 else last_lane)
                for b in range(fields):
                    shifted = edge if b == at else pltpu.roll(edge, (at - b) % 8, 0)
                    out[b, rows, :] = out[b, rows, :] + jnp.where(corner, shifted, 0.0)

    core = lax.rem(me, 2)
    sign = 2 * core - 1
    outward = jnp.logical_and(me + sign >= 0, me + sign < n)
    inward = jnp.logical_and(me - 2 * sign >= 0, me - 2 * sign < n)
    NEAR, SOLO, RELAY, MERGED = range(4)
    reach = (-sign, 2 * sign, -sign, sign)
    channel = (core, 3 - core, 2 + core, 1 - core)

    def pair_message(step, kind):
        rows = pl.ds(0, body + 8 if kind in (NEAR, MERGED) else body)
        return pltpu.make_async_remote_copy(
            src_ref=send.at[step, kind, rows],
            dst_ref=recv.at[step, kind, rows],
            send_sem=send_sem.at[step, kind],
            recv_sem=recv_sem.at[step, kind],
            device_id={"row": me + reach[kind]},
            device_id_type=MESH,
        )

    def permuted(parts, which):
        out = []
        for c in range(len(parts)):
            place = origin[which, pl.ds(8 * c, 8), :]
            low = jnp.bitwise_and(place, 7)
            high = jnp.right_shift(place, 3)
            total = jnp.take_along_axis(parts[0], low, axis=0)
            for k in range(1, len(parts)):
                total = jnp.where(high == k, jnp.take_along_axis(parts[k], low, axis=0), total)
            out.append(total)
        return out

    def fill(step, field, kind):
        chunks = tiles // 8
        slot = 3 + channel[kind]
        for b in range(fields):
            parts = []
            for c in range(chunks):
                rows = pl.ds(8 * c, 8)
                total = blk[slot, 0, b, rows, :] * field[0, rows, :]
                for a in range(1, fields):
                    total = total + blk[slot, a, b, rows, :] * field[a, rows, :]
                parts.append(total)
            if kind in (RELAY, MERGED):
                parts = permuted(parts, kind)
            for c in range(chunks):
                send[step, kind, pl.ds(b * tiles + 8 * c, 8), :] = parts[c]

    def edge_row(field, which):
        rows = pl.ds(tiles - 8 if which == 0 else 0, 8)
        at = 7 if which == 0 else 0
        values = [field[a, rows, :] for a in range(fields)]
        moved = product(values, lambda a, b: edge_blk[which, a, b])
        edge = jnp.zeros((8, cells), jnp.float32)
        for b in range(fields):
            shifted = moved[b] if b == at else pltpu.roll(moved[b], (b - at) % 8, 0)
            edge = jnp.where(row8 == b, shifted, edge)
        return pltpu.roll(edge, 1 if which == 0 else cells - 1, 1)

    def send_first(step, field):
        if step == 0:
            load(3 + channel[RELAY]).wait()
        fill(step, field, RELAY)
        if step == 0:
            pl.semaphore_wait(barrier, n - 1)

        @pl.when(inward)
        def _():
            pair_message(step, RELAY).start()

        if step == 0:
            load(3 + channel[SOLO]).wait()
        fill(step, field, SOLO)

        @pl.when(outward)
        def _():
            pair_message(step, SOLO).start()

        if step == 0:
            for which in range(2):
                edge_loads[which].wait()
        ahead, behind = edge_row(field, 0), edge_row(field, 1)
        first = core == 0
        send[step, NEAR, pl.ds(body, 8), :] = jnp.where(first, ahead, behind)
        send[step, MERGED, pl.ds(body, 8), :] = jnp.where(first, behind, ahead)
        if step == 0:
            load(3 + channel[MERGED]).wait()
        fill(step, field, MERGED)
        if step == 0:
            load(3 + channel[NEAR]).wait()
        fill(step, field, NEAR)
        pair_message(step, NEAR).start()

    def send_merged(step):
        @pl.when(outward)
        def _():
            pair_message(step, RELAY).wait_recv()
            send[step, MERGED, pl.ds(0, body), :] = (
                send[step, MERGED, pl.ds(0, body), :] + recv[step, RELAY, pl.ds(0, body), :]
            )
            pair_message(step, MERGED).start()

    def pair_receive(step, out):
        chunks = tiles // 8
        for kind in (NEAR, SOLO, MERGED):
            if kind == NEAR:
                pair_message(step, kind).wait_recv()
            else:
                @pl.when(inward if kind == SOLO else outward)
                def _():
                    pair_message(step, kind).wait_recv()

            for b in range(fields):
                parts = [
                    recv[step, kind, pl.ds(b * tiles + 8 * c, 8), :] for c in range(chunks)
                ]
                if kind != MERGED:
                    parts = permuted(parts, kind)
                for c in range(chunks):
                    rows = pl.ds(8 * c, 8)
                    out[b, rows, :] = out[b, rows, :] + parts[c]
        near, merged = recv[step, NEAR, pl.ds(body, 8), :], recv[step, MERGED, pl.ds(body, 8), :]
        first = core == 0
        for j in range(2):
            edge = jnp.where(first, merged, near) if j == 0 else jnp.where(first, near, merged)
            at = 0 if j == 0 else 7
            rows = pl.ds(0 if j == 0 else tiles - 8, 8)
            corner = jnp.logical_and(row8 == at, first_lane if j == 0 else last_lane)
            for b in range(fields):
                shifted = edge if b == at else pltpu.roll(edge, (at - b) % 8, 0)
                out[b, rows, :] = out[b, rows, :] + jnp.where(corner, shifted, 0.0)

    if paired:
        send_channels, send_rest, receive = send_first, send_merged, pair_receive
    else:
        send_rest = lambda step: None

    rank, team = lax.rem(me, group), me // group
    first_send, first_at, second_send, second_at = sums[:4], sums[4:8], sums[8:12], sums[12:]

    def first_copy(step, i, source):
        return pltpu.make_async_remote_copy(
            src_ref=first_send[step],
            dst_ref=first_at[step].at[source],
            send_sem=first_sems[0].at[step, i],
            recv_sem=first_sems[1].at[step, source],
            device_id={"row": team * group + lax.rem(rank + i, group)},
            device_id_type=MESH,
        )

    def second_copy(step, i, source):
        return pltpu.make_async_remote_copy(
            src_ref=second_send[step],
            dst_ref=second_at[step].at[source],
            send_sem=second_sems[0].at[step, i],
            recv_sem=second_sems[1].at[step, source],
            device_id={"row": lax.rem(me + i * group, n)},
            device_id_type=MESH,
        )

    def share(step, pairs):
        rows = [
            jnp.sum(jnp.sum(x * y, axis=0), axis=0, keepdims=True) for x, y in pairs
        ]
        row = jnp.concatenate(rows, axis=0)
        first_send[step][...] = row
        first_at[step][rank] = row
        for i in range(1, group):
            first_copy(step, i, rank).start()

    def pass_on(step):
        for i in range(1, group):
            first_copy(step, i, lax.rem(rank + i, group)).wait_recv()
        row = jnp.sum(first_at[step][...], axis=0)
        second_send[step][...] = row
        second_at[step][team] = row
        for i in range(1, n // group):
            second_copy(step, i, team).start()

    def collect(step, count):
        for i in range(1, n // group):
            second_copy(step, i, lax.rem(team + i, n // group)).wait_recv()
        total = jnp.sum(jnp.sum(second_at[step][...], axis=0), axis=1, keepdims=True)
        return [total[q:q + 1] for q in range(count)]

    b_load.wait()
    send_channels(0, b_ref)
    local_part(0, b_ref, img)
    send_rest(0)
    receive(0, img)
    b = b_ref[...]
    share(0, [(b, b), (b, img[...])])

    send_channels(1, img)
    local_part(1, img, img2)
    send_rest(1)
    pass_on(0)
    rho, shadow_image = collect(0, 2)
    alpha = rho / shadow_image
    receive(1, img2)
    half[...] = b_ref[...] - alpha * img[...]
    bent[...] = img[...] - alpha * img2[...]
    share(1, [
        (bent[...], half[...]), (bent[...], bent[...]),
        (b_ref[...], bent[...]), (b_ref[...], half[...]),
    ])

    send_channels(2, bent)
    local_part(2, bent, bent_img)
    send_rest(2)
    pass_on(1)
    tilt, square, shadow_bent, shadow_half = collect(1, 4)
    omega = tilt / square
    rho_next = shadow_half - omega * shadow_bent
    beta = rho_next / rho * (alpha / omega)
    adj_ref[...] = alpha * b_ref[...] + omega * half[...]
    res_ref[...] = half[...] - omega * bent[...]
    direc[...] = res_ref[...] + beta * (b_ref[...] - omega * img[...])
    img2[...] = bent[...] + beta * (img[...] - omega * img2[...])
    receive(2, bent_img)
    img[...] = img2[...] - omega * bent_img[...]
    share(2, [(b_ref[...], img[...])])

    send_channels(3, img)
    local_part(3, img, img2)
    send_rest(3)
    pass_on(2)
    (shadow_image,) = collect(2, 1)
    alpha = rho_next / shadow_image
    half[...] = res_ref[...] - alpha * img[...]
    bent[...] = bent[...] - omega * bent_img[...]
    adj_ref[...] = adj_ref[...] + alpha * direc[...]
    receive(3, img2)
    bent[...] = bent[...] - alpha * img2[...]
    share(3, [(bent[...], half[...]), (bent[...], bent[...])])
    pass_on(3)
    tilt, square = collect(3, 2)
    omega = tilt / square
    adj_ref[...] = adj_ref[...] + omega * half[...]
    res_ref[...] = half[...] - omega * bent[...]

    for step in range(4):
        if paired:
            pair_message(step, NEAR).wait_send()

            @pl.when(inward)
            def _():
                pair_message(step, RELAY).wait_send()

            @pl.when(outward)
            def _():
                pair_message(step, SOLO).wait_send()
                pair_message(step, MERGED).wait_send()
        else:
            for j in range(4):
                @pl.when(has_target(j))
                def _():
                    message(step, j).wait_send()

        for i in range(1, group):
            first_copy(step, i, rank).wait_send()
        for i in range(1, n // group):
            second_copy(step, i, team).wait_send()


def local(blocks, couplings, cotangent):
    tiles, slots, fields, _, cells = blocks.shape
    n = lax.axis_size("row")
    far = max(2, n // 8)
    group = n
    field = (fields, tiles, cells)
    f32 = jnp.float32
    vmem = pl.BlockSpec(memory_space=pltpu.VMEM)
    adjoint, residual = pl.pallas_call(
        functools.partial(kernel, n, far, group),
        out_shape=(jax.ShapeDtypeStruct(field, f32), jax.ShapeDtypeStruct(field, f32)),
        in_specs=[pl.BlockSpec(memory_space=pltpu.HBM)] * 3,
        out_specs=(vmem, vmem),
        scratch_shapes=[
            pltpu.VMEM((4, tiles), jnp.int32),
            pltpu.VMEM(field, f32),
            pltpu.VMEM((slots, fields, fields, tiles, cells), f32),
            pltpu.VMEM((2, fields, fields, 8, cells), f32),
            pltpu.VMEM((4, tiles, cells), jnp.int32),
        ]
        + [pltpu.VMEM(field, f32)] * 6
        + [
            pltpu.VMEM((4, 4, fields * tiles + 8, cells), f32),
            pltpu.VMEM((4, 4, fields * tiles + 8, cells), f32),
            pltpu.SemaphoreType.DMA((11,)),
            pltpu.SemaphoreType.DMA((4, 4)),
            pltpu.SemaphoreType.DMA((4, 4)),
            pltpu.SemaphoreType.DMA((4, group)),
            pltpu.SemaphoreType.DMA((4, group)),
            pltpu.SemaphoreType.DMA((4, n // group)),
            pltpu.SemaphoreType.DMA((4, n // group)),
        ]
        + [pltpu.VMEM((count, cells), f32) for count in SUMS]
        + [pltpu.VMEM((group, count, cells), f32) for count in SUMS]
        + [pltpu.VMEM((count, cells), f32) for count in SUMS]
        + [pltpu.VMEM((n // group, count, cells), f32) for count in SUMS],
        compiler_params=pltpu.CompilerParams(
            collective_id=0, has_side_effects=True, vmem_limit_bytes=50 * 1024 * 1024
        ),
        name="adjoint_solve",
    )(
        jnp.transpose(blocks, (1, 2, 3, 0, 4)),
        jnp.transpose(couplings),
        jnp.transpose(cotangent, (1, 0, 2)),
    )
    return jnp.transpose(adjoint, (1, 0, 2)), jnp.transpose(residual, (1, 0, 2))


def solution(mesh):
    placed = (
        P(("grp", "row"), None, None, None, None),
        P(("grp", "row"), None),
        P(("grp", "row"), None, None),
    )
    return jax.shard_map(
        local,
        mesh=mesh,
        in_specs=placed,
        out_specs=(P(("grp", "row"), None, None), P(("grp", "row"), None, None)),
        check_vma=False,
    )
```
